32 devices in a mesh: dp: 4 (over y, x), mp: 8 (over z, core).
Axes of the slice: x: 2, y: 2, z: 4, core: 2. Of those that a mesh axis runs over, the one named last changes fastest.
Arguments:
- residual: bfloat16 [1024, 4096], P(('dp', 'mp')), may hold values from -6 to 6
- ffn_gain: float32 [4096], replicated, may hold values from 0.5 to 1.5
- gate_weight: bfloat16 [4096, 8192], P(None, 'mp'), may hold values from -0.09375 to 0.09375
- up_weight: bfloat16 [4096, 8192], P(None, 'mp'), may hold values from -0.09375 to 0.09375
- down_weight: bfloat16 [8192, 4096], P('mp'), may hold values from -0.0625 to 0.0625
- final_gain: float32 [4096], replicated, may hold values from 0.5 to 1.5
- head_weight: bfloat16 [4096, 65536], P(None, 'mp')
- passage_ids: int32 [4, 256], P('dp'), may hold values from 0 to 3, never falling along the last dimension, each value on 1 to 128 neighbouring positions
- valid_counts: int32 [4, 4], P('dp'), may hold values from 1 to 128
Outputs:
- term_weights: float32 [16, 65536], P('dp', 'mp')
- entropy: float32 [], replicated
- grad_hidden: float32 [1024, 4096], P(('dp', 'mp'))
The draws below stay inside these ranges and needn't reach their ends.
Inputs may be any that keep to these rules, and one draw needn't show every extreme that they name: `passage_ids`: within each group the ids never fall and every passage of 0 to 3 has 1 to 128 rows.
All inputs are finite; a program needn't handle non-finite values.
Results may differ from the reference program's by a relative error of at most 0.0069.
The reference program's roundings to bfloat16 on the way (of `normed_in`, `activated`, `normed` and `slope_logit`) count: a program that leaves them out, or rounds other values in their place, can miss the bound.
Values may be sent and summed in bfloat16 or wider, within the bound.
A program may use at most 192 MiB of HBM per device.

```python
import math
import jax
import jax.numpy as jnp
import numpy as np
from jax import lax

D = 4096
FF = 8192
V = 65536
ROWS = 256
PASS = 4
MOST = 128
TOKENS = 1024
N_DP = 4


def draw_head_weight(key, part):
    column = jnp.arange(V, dtype=jnp.float32) / float(V - 1)
    entries = jax.random.truncated_normal(key, -6.0, 6.0, (D, V), jnp.float32)
    lowest = 0.5
    highest = 4.0
    column_scale = jnp.exp(math.log(lowest) + column * math.log(highest / lowest))
    values = entries * column_scale[None, :] * float(D) ** (-0.5)
    return values.astype(jnp.bfloat16)


def place_ends(array, own_key, smallest, high):
    dims = array.shape
    spot = [jax.random.randint(jax.random.fold_in(own_key, axis), (), 0, dims[axis]) for axis in range(len(dims))]
    array = array.at[tuple(spot)].set(smallest)
    longest = dims.index(max(dims))
    spot[longest] = (spot[longest] + 1) % dims[longest]
    return array.at[tuple(spot)].set(high)


def block_scale(key, extent, shards, least, high):
    loudness = 1.0
    for axis_at, blocks in shards:
        heights = jax.random.uniform(jax.random.fold_in(jax.random.fold_in(key, 6), axis_at), (blocks,), jnp.float32, least / len(shards), high / len(shards))
        loudness = loudness * jnp.repeat(jnp.exp(heights), extent[axis_at] // blocks).reshape((-1,) + (1,) * (len(extent) - 1 - axis_at))
    return loudness


def split_up(amount, total, limit, lean):
    weights = [(1 << 20) // math.isqrt(standing ** lean) + 1 for standing in range(2, amount + 1)]
    spare, given = total - limit - (amount - 1), [1] * (amount - 1)
    while spare > 0:
        free = [i for i in range(amount - 1) if given[i] < limit]
        mass, left = sum([weights[i] for i in free]), spare
        for i in free:
            more = min(limit - given[i], max(1, left * weights[i] // mass), spare)
            given[i] = given[i] + more
            spare = spare - more
    return np.array([limit] + given)


def uneven(key, count, total, most, skew):
    if count == 2:
        one = jax.random.randint(key, (), max(1, total - most), min(most, total - 1) + 1)
        return jnp.stack([one, total - one])
    lengths = jnp.asarray(split_up(count, total, most, skew), jnp.int32)
    twos = (count - 1) // 2
    giver, taker = lengths[1:1 + 2 * twos:2], lengths[2:2 + 2 * twos:2]
    room = jnp.minimum(giver - 1, most - taker)
    passed = jax.random.randint(jax.random.fold_in(key, 1), (twos,), 0, 1 << 20) % (room + 1)
    lengths = lengths.at[1:1 + 2 * twos:2].set(giver - passed).at[2:2 + 2 * twos:2].set(taker + passed)
    return lengths[jax.random.permutation(jax.random.fold_in(key, 2), count)]


def noise(key, dims, deviation, bound, split=(), held_as=jnp.bfloat16):
    array = deviation * jax.random.normal(key, dims, jnp.float32)
    if split:
        array = array * block_scale(key, dims, split, -0.22, 0.18)
    return jnp.clip(array, -bound, bound).astype(held_as)


def setup_inputs(seed: int = 0) -> dict:
    seeds = jax.random.split(jax.random.key(seed), 10)
    return {
        "residual": noise(seeds[0], (TOKENS, D), 1.0, 6.0, ((0, 32),)),
        "ffn_gain": jnp.clip(1.0 + 0.1 * jax.random.normal(seeds[1], (D,), jnp.float32), 0.5, 1.5),
        "gate_weight": noise(seeds[2], (D, FF), D ** -0.5, 0.09375, ((1, 8),)),
        "up_weight": noise(seeds[3], (D, FF), D ** -0.5, 0.09375, ((1, 8),)),
        "down_weight": noise(seeds[4], (FF, D), FF ** -0.5, 0.0625, ((0, 8),)),
        "final_gain": jnp.clip(1.0 + 0.1 * jax.random.normal(seeds[5], (D,), jnp.float32), 0.5, 1.5),
        "head_weight": draw_head_weight(jax.random.fold_in(seeds[9], 71), 0),
        "passage_ids": jax.vmap(lambda own: jnp.searchsorted(jnp.cumsum(uneven(own, PASS, ROWS, MOST, 1)), jnp.arange(ROWS), side="right"))(jax.random.split(seeds[7], N_DP)).reshape((N_DP, ROWS)).astype(jnp.int32),
        "valid_counts": place_ends(jax.random.randint(seeds[8], (N_DP, PASS), 1, MOST + 1), jax.random.fold_in(seeds[8], 1), 1, MOST).astype(jnp.int32),
    }


def rms_scale(values):
    return lax.rsqrt(lax.optimization_barrier(jnp.mean(values * values, axis=-1, keepdims=True)) + 1e-05)

def pool_masks(ids, counts):
    slots = jnp.arange(counts.shape[0], dtype=jnp.int32)
    member = ids[:, None] == slots[None, :]
    starts = lax.optimization_barrier(jnp.sum((ids[:, None] < slots[None, :]).astype(jnp.int32), axis=0))
    start_row = lax.optimization_barrier(jnp.sum(jnp.where(member, starts[None, :], 0), axis=1)).astype(jnp.int32)
    count_row = lax.optimization_barrier(jnp.sum(jnp.where(member, counts[None, :], 0), axis=1)).astype(jnp.int32)
    position = jnp.arange(ids.shape[0], dtype=jnp.int32) - start_row
    valid = (position < count_row).astype(jnp.float32)
    return (member.astype(jnp.float32), valid)

def reference(residual, ffn_gain, gate_weight, up_weight, down_weight, final_gain, head_weight, passage_ids, valid_counts):
    highest = lax.Precision.HIGHEST
    kept = []
    pooled_list = []
    for group_index in range(N_DP):
        row_block = residual[group_index * ROWS:(group_index + 1) * ROWS].astype(jnp.float32)
        normed_in = (row_block * rms_scale(row_block) * ffn_gain).astype(jnp.bfloat16)
        gate_vals = jnp.dot(normed_in, gate_weight, preferred_element_type=jnp.float32)
        up_vals = jnp.dot(normed_in, up_weight, preferred_element_type=jnp.float32)
        activated = (jax.nn.silu(gate_vals) * up_vals).astype(jnp.bfloat16)
        hidden = row_block + jnp.dot(activated, down_weight, preferred_element_type=jnp.float32)
        scale = rms_scale(hidden)
        normed = (hidden * scale * final_gain).astype(jnp.bfloat16)
        logits = jnp.dot(normed, head_weight, preferred_element_type=jnp.float32)
        member, valid = pool_masks(passage_ids[group_index], valid_counts[group_index])
        weights = jnp.log1p(jnp.maximum(logits, 0.0))
        powered = valid[:, None] * weights ** 4
        pooled_sum = jnp.dot(member.T, powered, precision=highest)
        kept.append((hidden, scale, logits, weights, member, valid, pooled_sum))
        pooled_list.append(pooled_sum)
    pooled_all = jnp.concatenate(pooled_list, axis=0)
    term_weights = (1.0 + pooled_all) ** 0.25 - 1.0
    smooth = 1.0 + lax.optimization_barrier(jnp.sum(term_weights, axis=0))
    total = jnp.sum(smooth)
    spread = jnp.sum(smooth * jnp.log(smooth))
    entropy = jnp.log(total) - spread / total
    slope_mass = jnp.log(total) - jnp.log(smooth)
    grads = []
    for hidden, scale, logits, weights, member, valid, pooled_sum in kept:
        factor = (1.0 + pooled_sum) ** (-0.75)
        row_factor = jnp.dot(member, factor, precision=highest)
        slope_logit = (valid[:, None] * weights ** 3 * row_factor * slope_mass[None, :] / (1.0 + jnp.maximum(logits, 0.0))).astype(jnp.bfloat16)
        slope_normed = jnp.dot(slope_logit, head_weight.T, preferred_element_type=jnp.float32)
        scaled_slope = slope_normed * final_gain
        grads.append(scale * scaled_slope - hidden * scale ** 3 * lax.optimization_barrier(jnp.mean(scaled_slope * hidden, axis=-1, keepdims=True)))
    grad_hidden = jnp.concatenate(grads, axis=0)
    return (term_weights, entropy, grad_hidden)
```

```python
import functools

import jax
import jax.numpy as jnp
from jax import lax
from jax.experimental import pallas as pl
from jax.experimental.pallas import tpu as pltpu
from jax.sharding import PartitionSpec as P

MIB = 1024 * 1024
MESH = pl.DeviceIdType.MESH


def place():
    dp, me = lax.axis_index("dp"), lax.axis_index("mp")
    return dp, me, lax.div(me, 2), lax.rem(me, 2)


def greet(chips):
    dp, me, chip, core = place()
    barrier = pltpu.get_barrier_semaphore()
    pl.semaphore_signal(barrier, inc=1, device_id=(dp, chip * 2 + 1 - core), device_id_type=MESH)
    for k in range(1, chips):
        peer = lax.rem(chip + k, chips) * 2 + core
        pl.semaphore_signal(barrier, inc=1, device_id=(dp, peer), device_id_type=MESH)
    pl.semaphore_wait(barrier, chips)


def normed_rows(values, gain):
    scale = lax.rsqrt(jnp.mean(values * values, axis=-1, keepdims=True) + 1e-05)
    return (values * scale * gain).astype(jnp.bfloat16)


def gather_blocks(chips, own, out, local_sem, z_send, z_recv, c_send, c_recv):
    dp, me, chip, core = place()
    twin = chip * 2 + 1 - core
    sends = []
    for k in range(1, chips):
        peer = lax.rem(chip + k, chips) * 2 + core
        copy = pltpu.make_async_remote_copy(
            src_ref=own, dst_ref=out.at[me], send_sem=z_send.at[k - 1], recv_sem=z_recv.at[k - 1],
            device_id=(dp, peer), device_id_type=MESH,
        )
        copy.start()
        sends.append(copy)
    first = pltpu.make_async_remote_copy(
        src_ref=own, dst_ref=out.at[me], send_sem=c_send.at[0], recv_sem=c_recv.at[0],
        device_id=(dp, twin), device_id_type=MESH,
    )
    first.start()
    local = pltpu.make_async_copy(own, out.at[me], local_sem)
    local.start()
    passed = [first]
    for k in sorted(range(1, chips), key=lambda k: min(k, chips - k)):
        source = lax.rem(chip + chips - k, chips) * 2 + core
        sends[k - 1].wait_recv()
        onward = pltpu.make_async_remote_copy(
            src_ref=out.at[source], dst_ref=out.at[source], send_sem=c_send.at[k], recv_sem=c_recv.at[k],
            device_id=(dp, twin), device_id_type=MESH,
        )
        onward.start()
        passed.append(onward)
    local.wait()
    for copy in sends:
        copy.wait_send()
    for copy in passed:
        copy.wait()


def gather_sems(chips):
    dma = pltpu.SemaphoreType.DMA
    return [dma, dma((chips - 1,)), dma((chips - 1,)), dma((chips,)), dma((chips,))]


def norm_gather_kernel(chips, rows_ref, gain_ref, out, own, *sems):
    own[...] = normed_rows(rows_ref[...].astype(jnp.float32), gain_ref[...])
    greet(chips)
    gather_blocks(chips, own, out, *sems)


def norm_gather(residual, gain, size):
    rows, width = residual.shape
    chips = size // 2
    return pl.pallas_call(
        functools.partial(norm_gather_kernel, chips),
        out_shape=jax.ShapeDtypeStruct((size, rows, width), jnp.bfloat16),
        in_specs=[pl.BlockSpec(memory_space=pltpu.VMEM)] * 2,
        out_specs=pl.BlockSpec(memory_space=pl.ANY),
        scratch_shapes=[pltpu.VMEM((rows, width), jnp.bfloat16)] + gather_sems(chips),
        compiler_params=pltpu.CompilerParams(
            collective_id=0, has_side_effects=True, vmem_limit_bytes=24 * MIB
        ),
    )(residual, gain.reshape(1, width))


def sum_norm_gather_kernel(
    chips, part, rows_ref, gain_ref, hidden_ref, out, own, pair, outgo, arrived,
    p_send, p_recv, s_send, s_recv, *sems,
):
    dp, me, chip, core = place()
    twin = chip * 2 + 1 - core
    greet(chips)
    order = list(range(1, chips)) + [0]
    swaps = {}
    for k in order:
        peer = lax.rem(chip + k, chips)
        swaps[k] = pltpu.make_async_remote_copy(
            src_ref=part.at[peer * 2 + 1 - core], dst_ref=pair.at[k],
            send_sem=p_send.at[k], recv_sem=p_recv.at[k],
            device_id=(dp, twin), device_id_type=MESH,
        )
        swaps[k].start()
    sends = []
    for k in order:
        peer = lax.rem(chip + k, chips)
        swaps[k].wait_recv()
        both = part[peer * 2 + core] + pair[k]
        if k == 0:
            hidden_ref[...] = both + rows_ref[...].astype(jnp.float32)
        else:
            outgo[k - 1] = both.astype(jnp.bfloat16)
            copy = pltpu.make_async_remote_copy(
                src_ref=outgo.at[k - 1], dst_ref=arrived.at[k - 1],
                send_sem=s_send.at[k - 1], recv_sem=s_recv.at[k - 1],
                device_id=(dp, peer * 2 + core), device_id_type=MESH,
            )
            copy.start()
            sends.append(copy)
    for copy in sends:
        copy.wait_recv()
    hidden = hidden_ref[...]
    for k in range(chips - 1):
        hidden = hidden + arrived[k].astype(jnp.float32)
    hidden_ref[...] = hidden
    own[...] = normed_rows(hidden, gain_ref[...])
    gather_blocks(chips, own, out, *sems)
    for copy in sends:
        copy.wait_send()
    for k in order:
        swaps[k].wait_send()


def sum_norm_gather(part, residual, gain, size):
    rows, width = residual.shape
    chips = size // 2
    dma = pltpu.SemaphoreType.DMA
    return pl.pallas_call(
        functools.partial(sum_norm_gather_kernel, chips),
        out_shape=(
            jax.ShapeDtypeStruct((rows, width), jnp.float32),
            jax.ShapeDtypeStruct((size, rows, width), jnp.bfloat16),
        ),
        in_specs=[pl.BlockSpec(memory_space=pltpu.VMEM)] * 3,
        out_specs=(pl.BlockSpec(memory_space=pltpu.VMEM), pl.BlockSpec(memory_space=pl.ANY)),
        scratch_shapes=[
            pltpu.VMEM((rows, width), jnp.bfloat16),
            pltpu.VMEM((chips, rows, width), jnp.float32),
            pltpu.VMEM((chips - 1, rows, width), jnp.bfloat16),
            pltpu.VMEM((chips - 1, rows, width), jnp.bfloat16),
            dma((chips,)), dma((chips,)), dma((chips - 1,)), dma((chips - 1,)),
        ] + gather_sems(chips),
        compiler_params=pltpu.CompilerParams(
            collective_id=1, has_side_effects=True, vmem_limit_bytes=32 * MIB
        ),
    )(part.reshape(size, rows, width), residual, gain.reshape(1, width))


def slope_kernel(
    chips, steps, deep, slope, head, hidden_ref, gain_ref, grad_ref, total, part, pair, outgo, arrived,
    p_send, p_recv, s_send, s_recv,
):
    dp, me, chip, core = place()
    twin = chip * 2 + 1 - core
    rows = hidden_ref.shape[0]
    wide = head.shape[0]
    step = pl.program_id(0)

    @pl.when(step == 0)
    def _():
        greet(chips)

    total[...] = jnp.zeros_like(total)

    @pl.loop(0, slope.shape[1] // deep)
    def _(at):
        span = pl.ds(pl.multiple_of(at * deep, deep), deep)
        total[...] += lax.dot_general(
            slope[:, span], head[:, span], (((1,), (1,)), ((), ())),
            preferred_element_type=jnp.float32,
        )

    for z in range(chips):
        for c in range(2):
            block = z * 2 + c
            part[step, c, z] = total[block * rows:(block + 1) * rows, :]

    def swap(at):
        return pltpu.make_async_remote_copy(
            src_ref=part.at[at, 1 - core], dst_ref=pair.at[at],
            send_sem=p_send.at[at], recv_sem=p_recv.at[at],
            device_id=(dp, twin), device_id_type=MESH,
        )

    def send(at, k):
        peer = lax.rem(chip + k, chips)
        return pltpu.make_async_remote_copy(
            src_ref=outgo.at[at, k - 1], dst_ref=arrived.at[at, k - 1],
            send_sem=s_send.at[at, k - 1], recv_sem=s_recv.at[at, k - 1],
            device_id=(dp, peer * 2 + core), device_id_type=MESH,
        )

    def forward(at):
        swap(at).wait_recv()
        for k in range(1, chips):
            peer = lax.rem(chip + k, chips)
            outgo[at, k - 1] = (part[at, core, peer] + pair[at, peer]).astype(jnp.bfloat16)
            send(at, k).start()

    swap(step).start()

    @pl.when(step > 0)
    def _():
        forward(step - 1)

    @pl.when(step == steps - 1)
    def _():
        forward(steps - 1)
        hidden = hidden_ref[...]
        scale = lax.rsqrt(jnp.mean(hidden * hidden, axis=-1, keepdims=True) + 1e-05)
        inner = jnp.zeros((rows, 1), jnp.float32)
        for at in range(steps):
            span = slice(at * wide, (at + 1) * wide)
            value = part[at, core, chip] + pair[at, chip]
            for k in range(1, chips):
                send(at, k).wait_recv()
                value = value + arrived[at, k - 1].astype(jnp.float32)
            value = value * gain_ref[:, span]
            grad_ref[:, span] = value
            inner = inner + jnp.sum(value * hidden_ref[:, span], axis=-1, keepdims=True)
        inner = inner / (steps * wide)
        grad_ref[...] = scale * grad_ref[...] - hidden_ref[...] * (scale * scale * scale * inner)
        for at in range(steps):
            swap(at).wait_send()
            for k in range(1, chips):
                send(at, k).wait_send()


def slope_grad(slope, head, hidden, gain, size):
    rows, width = hidden.shape
    group, vocab = slope.shape
    chips = size // 2
    wide = min(512, width)
    steps = width // wide
    deep = min(2048, vocab)
    dma = pltpu.SemaphoreType.DMA
    return pl.pallas_call(
        functools.partial(slope_kernel, chips, steps, deep),
        grid=(steps,),
        out_shape=jax.ShapeDtypeStruct((rows, width), jnp.float32),
        in_specs=[
            pl.BlockSpec((group, vocab), lambda i: (0, 0)),
            pl.BlockSpec((wide, vocab), lambda i: (i, 0)),
            pl.BlockSpec((rows, width), lambda i: (0, 0)),
            pl.BlockSpec((1, width), lambda i: (0, 0)),
        ],
        out_specs=pl.BlockSpec((rows, width), lambda i: (0, 0)),
        scratch_shapes=[
            pltpu.VMEM((group, wide), jnp.float32),
            pltpu.VMEM((steps, 2, chips, rows, wide), jnp.float32),
            pltpu.VMEM((steps, chips, rows, wide), jnp.float32),
            pltpu.VMEM((steps, chips - 1, rows, wide), jnp.bfloat16),
            pltpu.VMEM((steps, chips - 1, rows, wide), jnp.bfloat16),
            dma((steps,)), dma((steps,)), dma((steps, chips - 1)), dma((steps, chips - 1)),
        ],
        compiler_params=pltpu.CompilerParams(
            collective_id=2, has_side_effects=True, vmem_limit_bytes=48 * MIB
        ),
    )(slope, head, hidden, gain.reshape(1, width))


def rms_scale(values):
    return lax.rsqrt(jnp.mean(values * values, axis=-1, keepdims=True) + 1e-05)


def pool_masks(ids, counts):
    slots = jnp.arange(counts.shape[0], dtype=jnp.int32)
    member = ids[:, None] == slots[None, :]
    starts = jnp.sum((ids[:, None] < slots[None, :]).astype(jnp.int32), axis=0)
    start_row = jnp.sum(jnp.where(member, starts[None, :], 0), axis=1)
    count_row = jnp.sum(jnp.where(member, counts[None, :], 0), axis=1)
    position = jnp.arange(ids.shape[0], dtype=jnp.int32) - start_row
    valid = (position < count_row).astype(jnp.float32)
    return (member.astype(jnp.float32), valid)


def body(
    line,
    residual,
    ffn_gain,
    gate_weight,
    up_weight,
    down_weight,
    final_gain,
    head_weight,
    passage_ids,
    valid_counts,
):
    highest = lax.Precision.HIGHEST
    tok_rows, width = residual.shape
    size = lax.axis_size("mp")
    group_rows = tok_rows * size
    if line:
        gathered = norm_gather(residual, ffn_gain, size).reshape(group_rows, width)
    else:
        own_rows = residual.astype(jnp.float32)
        normed_in = (own_rows * rms_scale(own_rows) * ffn_gain).astype(jnp.bfloat16)
        gathered = lax.all_gather(normed_in, "mp", axis=0, tiled=True)
    gate_vals = jnp.dot(gathered, gate_weight, preferred_element_type=jnp.float32)
    up_vals = jnp.dot(gathered, up_weight, preferred_element_type=jnp.float32)
    activated = (jax.nn.silu(gate_vals) * up_vals).astype(jnp.bfloat16)
    part = jnp.dot(activated, down_weight, preferred_element_type=jnp.float32)
    if line:
        hidden, normed_all = sum_norm_gather(part, residual, final_gain, size)
        normed_all = normed_all.reshape(group_rows, width)
    else:
        hidden = own_rows + lax.psum_scatter(part, "mp", scatter_dimension=0, tiled=True)
        normed = (hidden * rms_scale(hidden) * final_gain).astype(jnp.bfloat16)
        normed_all = lax.all_gather(normed, "mp", axis=0, tiled=True)
    logits = jnp.dot(normed_all, head_weight, preferred_element_type=jnp.float32)
    member, valid = pool_masks(passage_ids[0], valid_counts[0])
    weights = jnp.log1p(jnp.maximum(logits, 0.0))
    powered = valid[:, None] * weights**4
    pooled_sum = lax.dot_general(member, powered, (((0,), (0,)), ((), ())), precision=highest)
    term_weights = (1.0 + pooled_sum) ** 0.25 - 1.0
    local_mass = jnp.sum(term_weights, axis=0)
    entries = local_mass.shape[0] * size
    smooth = 1.0 + lax.psum(local_mass, "dp")
    total = entries + lax.psum(jnp.sum(local_mass), ("dp", "mp"))
    slope_mass = jnp.log(total) - jnp.log(smooth)
    factor = (1.0 + pooled_sum) ** (-0.75)
    row_factor = jnp.dot(member, factor, precision=highest)
    slope_logit = (
        valid[:, None]
        * weights**3
        * row_factor
        * slope_mass[None, :]
        / (1.0 + jnp.maximum(logits, 0.0))
    ).astype(jnp.bfloat16)
    if line:
        grad_hidden = slope_grad(slope_logit, head_weight, hidden, final_gain, size)
    else:
        slope_normed = lax.psum_scatter(
            lax.dot_general(
                slope_logit, head_weight, (((1,), (1,)), ((), ())), preferred_element_type=jnp.float32
            ),
            "mp",
            scatter_dimension=0,
            tiled=True,
        )
        scale = rms_scale(hidden)
        scaled_slope = slope_normed * final_gain
        grad_hidden = scale * scaled_slope - hidden * scale**3 * jnp.mean(
            scaled_slope * hidden, axis=-1, keepdims=True
        )
    spread = lax.psum(jnp.sum(smooth * jnp.log(smooth)), "mp")
    entropy = jnp.log(total) - spread / total
    return (term_weights, entropy, grad_hidden)


def solution(mesh):
    placed = (
        P(("dp", "mp"), None),
        P(),
        P(None, "mp"),
        P(None, "mp"),
        P("mp", None),
        P(),
        P(None, "mp"),
        P("dp", None),
        P("dp", None),
    )
    line = mesh.shape["mp"] == 8
    return jax.shard_map(
        functools.partial(body, line),
        mesh=mesh,
        in_specs=placed,
        out_specs=(P("dp", "mp"), P(), P(("dp", "mp"), None)),
        check_vma=False,
    )
```

```python
import functools

import jax
import jax.numpy as jnp
from jax import lax
from jax.experimental import pallas as pl
from jax.experimental.pallas import tpu as pltpu
from jax.sharding import PartitionSpec as P

MIB = 1024 * 1024
MESH = pl.DeviceIdType.MESH


def place():
    dp, me = lax.axis_index("dp"), lax.axis_index("mp")
    return dp, me, lax.div(me, 2), lax.rem(me, 2)


def greet(chips):
    dp, me, chip, core = place()
    barrier = pltpu.get_barrier_semaphore()
    pl.semaphore_signal(barrier, inc=1, device_id=(dp, chip * 2 + 1 - core), device_id_type=MESH)
    for k in range(1, chips):
        peer = lax.rem(chip + k, chips) * 2 + core
        pl.semaphore_signal(barrier, inc=1, device_id=(dp, peer), device_id_type=MESH)
    pl.semaphore_wait(barrier, chips)


def normed_rows(values, gain):
    scale = lax.rsqrt(jnp.mean(values * values, axis=-1, keepdims=True) + 1e-05)
    return (values * scale * gain).astype(jnp.bfloat16)


def gather_blocks(chips, own, out, local_sem, z_send, z_recv, c_send, c_recv):
    dp, me, chip, core = place()
    twin = chip * 2 + 1 - core
    sends = []
    for k in range(1, chips):
        peer = lax.rem(chip + k, chips) * 2 + core
        copy = pltpu.make_async_remote_copy(
            src_ref=own, dst_ref=out.at[me], send_sem=z_send.at[k - 1], recv_sem=z_recv.at[k - 1],
            device_id=(dp, peer), device_id_type=MESH,
        )
        copy.start()
        sends.append(copy)
    first = pltpu.make_async_remote_copy(
        src_ref=own, dst_ref=out.at[me], send_sem=c_send.at[0], recv_sem=c_recv.at[0],
        device_id=(dp, twin), device_id_type=MESH,
    )
    first.start()
    local = pltpu.make_async_copy(own, out.at[me], local_sem)
    local.start()
    passed = [first]
    for k in sorted(range(1, chips), key=lambda k: min(k, chips - k)):
        source = lax.rem(chip + chips - k, chips) * 2 + core
        sends[k - 1].wait_recv()
        onward = pltpu.make_async_remote_copy(
            src_ref=out.at[source], dst_ref=out.at[source], send_sem=c_send.at[k], recv_sem=c_recv.at[k],
            device_id=(dp, twin), device_id_type=MESH,
        )
        onward.start()
        passed.append(onward)
    local.wait()
    for copy in sends:
        copy.wait_send()
    for copy in passed:
        copy.wait()


def gather_sems(chips):
    dma = pltpu.SemaphoreType.DMA
    return [dma, dma((chips - 1,)), dma((chips - 1,)), dma((chips,)), dma((chips,))]


def norm_gather_kernel(chips, rows_ref, gain_ref, out, own, *sems):
    own[...] = normed_rows(rows_ref[...].astype(jnp.float32), gain_ref[...])
    greet(chips)
    gather_blocks(chips, own, out, *sems)


def norm_gather(residual, gain, size):
    rows, width = residual.shape
    chips = size // 2
    return pl.pallas_call(
        functools.partial(norm_gather_kernel, chips),
        out_shape=jax.ShapeDtypeStruct((size, rows, width), jnp.bfloat16),
        in_specs=[pl.BlockSpec(memory_space=pltpu.VMEM)] * 2,
        out_specs=pl.BlockSpec(memory_space=pl.ANY),
        scratch_shapes=[pltpu.VMEM((rows, width), jnp.bfloat16)] + gather_sems(chips),
        compiler_params=pltpu.CompilerParams(
            collective_id=0, has_side_effects=True, vmem_limit_bytes=24 * MIB
        ),
    )(residual, gain.reshape(1, width))


def sum_norm_gather_kernel(
    chips, part, rows_ref, gain_ref, hidden_ref, out, own, pair, outgo, arrived,
    p_send, p_recv, s_send, s_recv, *sems,
):
    dp, me, chip, core = place()
    twin = chip * 2 + 1 - core
    greet(chips)
    order = list(range(1, chips)) + [0]
    swaps = {}
    for k in order:
        peer = lax.rem(chip + k, chips)
        swaps[k] = pltpu.make_async_remote_copy(
            src_ref=part.at[peer * 2 + 1 - core], dst_ref=pair.at[k],
            send_sem=p_send.at[k], recv_sem=p_recv.at[k],
            device_id=(dp, twin), device_id_type=MESH,
        )
        swaps[k].start()
    sends = []
    for k in order:
        peer = lax.rem(chip + k, chips)
        swaps[k].wait_recv()
        both = part[peer * 2 + core] + pair[k]
        if k == 0:
            hidden_ref[...] = both + rows_ref[...].astype(jnp.float32)
        else:
            outgo[k - 1] = both.astype(jnp.bfloat16)
            copy = pltpu.make_async_remote_copy(
                src_ref=outgo.at[k - 1], dst_ref=arrived.at[k - 1],
                send_sem=s_send.at[k - 1], recv_sem=s_recv.at[k - 1],
                device_id=(dp, peer * 2 + core), device_id_type=MESH,
            )
            copy.start()
            sends.append(copy)
    for copy in sends:
        copy.wait_recv()
    hidden = hidden_ref[...]
    for k in range(chips - 1):
        hidden = hidden + arrived[k].astype(jnp.float32)
    hidden_ref[...] = hidden
    own[...] = normed_rows(hidden, gain_ref[...])
    gather_blocks(chips, own, out, *sems)
    for copy in sends:
        copy.wait_send()
    for k in order:
        swaps[k].wait_send()


def sum_norm_gather(part, residual, gain, size):
    rows, width = residual.shape
    chips = size // 2
    dma = pltpu.SemaphoreType.DMA
    return pl.pallas_call(
        functools.partial(sum_norm_gather_kernel, chips),
        out_shape=(
            jax.ShapeDtypeStruct((rows, width), jnp.float32),
            jax.ShapeDtypeStruct((size, rows, width), jnp.bfloat16),
        ),
        in_specs=[pl.BlockSpec(memory_space=pltpu.VMEM)] * 3,
        out_specs=(pl.BlockSpec(memory_space=pltpu.VMEM), pl.BlockSpec(memory_space=pl.ANY)),
        scratch_shapes=[
            pltpu.VMEM((rows, width), jnp.bfloat16),
            pltpu.VMEM((chips, rows, width), jnp.float32),
            pltpu.VMEM((chips - 1, rows, width), jnp.bfloat16),
            pltpu.VMEM((chips - 1, rows, width), jnp.bfloat16),
            dma((chips,)), dma((chips,)), dma((chips - 1,)), dma((chips - 1,)),
        ] + gather_sems(chips),
        compiler_params=pltpu.CompilerParams(
            collective_id=1, has_side_effects=True, vmem_limit_bytes=32 * MIB
        ),
    )(part.reshape(size, rows, width), residual, gain.reshape(1, width))


def slope_kernel(
    chips, steps, deep, slope, head, hidden_ref, gain_ref, grad_ref, total, part, pair, outgo, arrived,
    p_send, p_recv, s_send, s_recv,
):
    dp, me, chip, core = place()
    twin = chip * 2 + 1 - core
    rows = hidden_ref.shape[0]
    wide = head.shape[0]
    step = pl.program_id(0)

    @pl.when(step == 0)
    def _():
        greet(chips)

    total[...] = jnp.zeros_like(total)

    @pl.loop(0, slope.shape[1] // deep)
    def _(at):
        span = pl.ds(pl.multiple_of(at * deep, deep), deep)
        total[...] += lax.dot_general(
            slope[:, span], head[:, span], (((1,), (1,)), ((), ())),
            preferred_element_type=jnp.float32,
        )

    for z in range(chips):
        for c in range(2):
            block = z * 2 + c
            part[step, c, z] = total[block * rows:(block + 1) * rows, :]

    def swap(at):
        return pltpu.make_async_remote_copy(
            src_ref=part.at[at, 1 - core], dst_ref=pair.at[at],
            send_sem=p_send.at[at], recv_sem=p_recv.at[at],
            device_id=(dp, twin), device_id_type=MESH,
        )

    def send(at, k):
        peer = lax.rem(chip + k, chips)
        return pltpu.make_async_remote_copy(
            src_ref=outgo.at[at, k - 1], dst_ref=arrived.at[at, k - 1],
            send_sem=s_send.at[at, k - 1], recv_sem=s_recv.at[at, k - 1],
            device_id=(dp, peer * 2 + core), device_id_type=MESH,
        )

    def forward(at):
        swap(at).wait_recv()
        for k in range(1, chips):
            peer = lax.rem(chip + k, chips)
            outgo[at, k - 1] = (part[at, core, peer] + pair[at, peer]).astype(jnp.bfloat16)
            send(at, k).start()

    swap(step).start()

    @pl.when(step > 0)
    def _():
        forward(step - 1)

    @pl.when(step == steps - 1)
    def _():
        forward(steps - 1)
        hidden = hidden_ref[...]
        scale = lax.rsqrt(jnp.mean(hidden * hidden, axis=-1, keepdims=True) + 1e-05)
        inner = jnp.zeros((rows, 1), jnp.float32)
        for at in range(steps):
            span = slice(at * wide, (at + 1) * wide)
            value = part[at, core, chip] + pair[at, chip]
            for k in range(1, chips):
                send(at, k).wait_recv()
                value = value + arrived[at, k - 1].astype(jnp.float32)
            value = value * gain_ref[:, span]
            grad_ref[:, span] = value
            inner = inner + jnp.sum(value * hidden_ref[:, span], axis=-1, keepdims=True)
        inner = inner / (steps * wide)
        grad_ref[...] = scale * grad_ref[...] - hidden_ref[...] * (scale * scale * scale * inner)
        for at in range(steps):
            swap(at).wait_send()
            for k in range(1, chips):
                send(at, k).wait_send()


def slope_grad(slope, head, hidden, gain, size):
    rows, width = hidden.shape
    group, vocab = slope.shape
    chips = size // 2
    wide = min(512, width)
    steps = width // wide
    deep = min(2048, vocab)
    dma = pltpu.SemaphoreType.DMA
    return pl.pallas_call(
        functools.partial(slope_kernel, chips, steps, deep),
        grid=(steps,),
        out_shape=jax.ShapeDtypeStruct((rows, width), jnp.float32),
        in_specs=[
            pl.BlockSpec((group, vocab), lambda i: (0, 0)),
            pl.BlockSpec((wide, vocab), lambda i: (i, 0)),
            pl.BlockSpec((rows, width), lambda i: (0, 0)),
            pl.BlockSpec((1, width), lambda i: (0, 0)),
        ],
        out_specs=pl.BlockSpec((rows, width), lambda i: (0, 0)),
        scratch_shapes=[
            pltpu.VMEM((group, wide), jnp.float32),
            pltpu.VMEM((steps, 2, chips, rows, wide), jnp.float32),
            pltpu.VMEM((steps, chips, rows, wide), jnp.float32),
            pltpu.VMEM((steps, chips - 1, rows, wide), jnp.bfloat16),
            pltpu.VMEM((steps, chips - 1, rows, wide), jnp.bfloat16),
            dma((steps,)), dma((steps,)), dma((steps, chips - 1)), dma((steps, chips - 1)),
        ],
        compiler_params=pltpu.CompilerParams(
            collective_id=2, has_side_effects=True, vmem_limit_bytes=48 * MIB
        ),
    )(slope, head, hidden, gain.reshape(1, width))


def all_sum_kernel(axis, size, own, out, slots, sends, recvs):
    dp, mp = lax.axis_index("dp"), lax.axis_index("mp")
    me = lax.axis_index(axis)

    def device(k):
        peer = lax.rem(me + k, size)
        return (peer, mp) if axis == "dp" else (dp, peer)

    slots[me] = own[...]
    barrier = pltpu.get_barrier_semaphore()
    for k in range(1, size):
        pl.semaphore_signal(barrier, inc=1, device_id=device(k), device_id_type=MESH)
    pl.semaphore_wait(barrier, size - 1)
    copies = []
    for k in range(1, size):
        copy = pltpu.make_async_remote_copy(
            src_ref=own, dst_ref=slots.at[me], send_sem=sends.at[k - 1], recv_sem=recvs.at[k - 1],
            device_id=device(k), device_id_type=MESH,
        )
        copy.start()
        copies.append(copy)
    for copy in copies:
        copy.wait()
    total = slots[0]
    for at in range(1, size):
        total = total + slots[at]
    out[...] = total


def all_sum(values, axis, number):
    size = lax.axis_size(axis)
    dma = pltpu.SemaphoreType.DMA
    return pl.pallas_call(
        functools.partial(all_sum_kernel, axis, size),
        out_shape=jax.ShapeDtypeStruct(values.shape, jnp.float32),
        in_specs=[pl.BlockSpec(memory_space=pltpu.VMEM)],
        out_specs=pl.BlockSpec(memory_space=pltpu.VMEM),
        scratch_shapes=[
            pltpu.VMEM((size,) + values.shape, jnp.float32), dma((size - 1,)), dma((size - 1,)),
        ],
        compiler_params=pltpu.CompilerParams(collective_id=number, has_side_effects=True),
    )(values)


def rms_scale(values):
    return lax.rsqrt(jnp.mean(values * values, axis=-1, keepdims=True) + 1e-05)


def pool_masks(ids, counts):
    slots = jnp.arange(counts.shape[0], dtype=jnp.int32)
    member = ids[:, None] == slots[None, :]
    starts = jnp.sum((ids[:, None] < slots[None, :]).astype(jnp.int32), axis=0)
    start_row = jnp.sum(jnp.where(member, starts[None, :], 0), axis=1)
    count_row = jnp.sum(jnp.where(member, counts[None, :], 0), axis=1)
    position = jnp.arange(ids.shape[0], dtype=jnp.int32) - start_row
    valid = (position < count_row).astype(jnp.float32)
    return (member.astype(jnp.float32), valid)


def body(
    line,
    residual,
    ffn_gain,
    gate_weight,
    up_weight,
    down_weight,
    final_gain,
    head_weight,
    passage_ids,
    valid_counts,
):
    highest = lax.Precision.HIGHEST
    tok_rows, width = residual.shape
    size = lax.axis_size("mp")
    group_rows = tok_rows * size
    if line:
        gathered = norm_gather(residual, ffn_gain, size).reshape(group_rows, width)
    else:
        own_rows = residual.astype(jnp.float32)
        normed_in = (own_rows * rms_scale(own_rows) * ffn_gain).astype(jnp.bfloat16)
        gathered = lax.all_gather(normed_in, "mp", axis=0, tiled=True)
    gate_vals = jnp.dot(gathered, gate_weight, preferred_element_type=jnp.float32)
    up_vals = jnp.dot(gathered, up_weight, preferred_element_type=jnp.float32)
    activated = (jax.nn.silu(gate_vals) * up_vals).astype(jnp.bfloat16)
    part = jnp.dot(activated, down_weight, preferred_element_type=jnp.float32)
    if line:
        hidden, normed_all = sum_norm_gather(part, residual, final_gain, size)
        normed_all = normed_all.reshape(group_rows, width)
    else:
        hidden = own_rows + lax.psum_scatter(part, "mp", scatter_dimension=0, tiled=True)
        normed = (hidden * rms_scale(hidden) * final_gain).astype(jnp.bfloat16)
        normed_all = lax.all_gather(normed, "mp", axis=0, tiled=True)
    logits = jnp.dot(normed_all, head_weight, preferred_element_type=jnp.float32)
    member, valid = pool_masks(passage_ids[0], valid_counts[0])
    weights = jnp.log1p(jnp.maximum(logits, 0.0))
    powered = valid[:, None] * weights**4
    pooled_sum = lax.dot_general(member, powered, (((0,), (0,)), ((), ())), precision=highest)
    term_weights = (1.0 + pooled_sum) ** 0.25 - 1.0
    local_mass = jnp.sum(term_weights, axis=0)
    if line:
        smooth = 1.0 + all_sum(local_mass.reshape(-1, 128), "dp", 3)
        tiles = smooth.reshape(-1, 8, 128)
        sums = jnp.stack([jnp.sum(tiles, axis=0), jnp.sum(tiles * jnp.log(tiles), axis=0)])
        total, spread = jnp.sum(all_sum(sums, "mp", 4), axis=(1, 2))
        smooth = smooth.reshape(-1)
    else:
        smooth = 1.0 + lax.psum(local_mass, "dp")
        total, spread = lax.psum((jnp.sum(smooth), jnp.sum(smooth * jnp.log(smooth))), "mp")
    slope_mass = jnp.log(total) - jnp.log(smooth)
    factor = (1.0 + pooled_sum) ** (-0.75)
    row_factor = jnp.dot(member, factor, precision=highest)
    slope_logit = (
        valid[:, None]
        * weights**3
        * row_factor
        * slope_mass[None, :]
        / (1.0 + jnp.maximum(logits, 0.0))
    ).astype(jnp.bfloat16)
    if line:
        grad_hidden = slope_grad(slope_logit, head_weight, hidden, final_gain, size)
    else:
        slope_normed = lax.psum_scatter(
            lax.dot_general(
                slope_logit, head_weight, (((1,), (1,)), ((), ())), preferred_element_type=jnp.float32
            ),
            "mp",
            scatter_dimension=0,
            tiled=True,
        )
        scale = rms_scale(hidden)
        scaled_slope = slope_normed * final_gain
        grad_hidden = scale * scaled_slope - hidden * scale**3 * jnp.mean(
            scaled_slope * hidden, axis=-1, keepdims=True
        )
    entropy = jnp.log(total) - spread / total
    return (term_weights, entropy, grad_hidden)


def solution(mesh):
    placed = (
        P(("dp", "mp"), None),
        P(),
        P(None, "mp"),
        P(None, "mp"),
        P("mp", None),
        P(),
        P(None, "mp"),
        P("dp", None),
        P("dp", None),
    )
    line = mesh.shape["mp"] == 8
    return jax.shard_map(
        functools.partial(body, line),
        mesh=mesh,
        in_specs=placed,
        out_specs=(P("dp", "mp"), P(), P(("dp", "mp"), None)),
        check_vma=False,
    )
```
